512 devices in a mesh: rep: 16 (over y_hi, x, core), fsdp: 32 (over z, y_lo).
Axes of the slice: x: 4, y: 8 (y_hi: 2, y_lo: 4; y = y_hi * 4 + y_lo), z: 8, core: 2. Of those that a mesh axis runs over, the one named last changes fastest.
Arguments:
- deltas: float32 [16, 4194304], P('rep', 'fsdp'), may hold values from -45 to 45
- noise_first: float32 [16, 4194304], P('rep', 'fsdp'), may hold values from 0 to 1
- params: float32 [4194304], P('fsdp'), may hold values from -6 to 6
- momentum: float32 [4194304], P('fsdp'), may hold values from -6 to 6
- noise_second: float32 [4194304], P('fsdp'), may hold values from 0 to 1
Outputs:
- new_params: float32 [4194304], P('fsdp')
- new_momentum: float32 [4194304], P('fsdp')
The draws below stay inside these ranges and needn't reach their ends.
All inputs are finite; a program needn't handle non-finite values.
Results may differ from the reference program's by a relative error of at most 0.0003.
Values may be sent and summed in bfloat16 or wider, within the bound.
No kernel may reach another device: no remote copies, remote signals or barrier semaphores. Data moves between devices by JAX's collectives and lax.ppermute only.
A program may use at most 64 MiB of HBM per device.

```python
import jax
import jax.numpy as jnp
import numpy as np
from jax import lax

PARAM_DEV = 131072
BLOCK = 32
LEVELS = 8
REPLICAS = 16
PARAMS = 4194304


def draw_deltas(key, part):
    block_key, own_key, common_key, mixing_key, height_key = jax.random.split(jax.random.fold_in(key, 11), 5)
    shard_count = PARAMS // PARAM_DEV
    block_count = PARAMS // BLOCK
    block_scale = jnp.exp(jax.random.uniform(block_key, (block_count,), jnp.float32) * jnp.log(10.0))
    block_scale = jnp.repeat(block_scale, BLOCK)
    ramp_up = 3.0 ** (jnp.arange(PARAMS, dtype=jnp.float32) / PARAMS)
    heights = jnp.exp(jax.random.uniform(height_key, (shard_count,), jnp.float32) * jnp.log(3.0))
    height_rows = jnp.repeat(heights, PARAM_DEV)
    common_part = jnp.clip(jax.random.normal(common_key, (1, PARAMS), jnp.float32), -5.0, 5.0)
    mixing = jax.random.uniform(mixing_key, (shard_count,), jnp.float32, 0.0, 1.0)
    own_part = jnp.clip(jax.random.normal(own_key, (REPLICAS, PARAMS), jnp.float32), -5.0, 5.0)
    mixing_rows = jnp.repeat(mixing, PARAM_DEV)[None, :]
    base_draw = jnp.clip(mixing_rows * common_part + jnp.sqrt(1.0 - mixing_rows * mixing_rows) * own_part, -5.0, 5.0)
    scale_rows = block_scale * ramp_up * height_rows
    return (0.1 * base_draw * scale_rows[None, :]).astype(jnp.float32)


def shard_levels(rng, shape, cuts, smallest, high):
    factor_of, own = 1.0, jax.random.fold_in(rng, 6)
    for axis_at, parts in cuts:
        steps = jnp.exp(jax.random.uniform(jax.random.fold_in(own, axis_at), (parts,), jnp.float32, smallest / len(cuts), high / len(cuts)))
        factor_of = factor_of * jnp.repeat(steps, shape[axis_at] // parts).reshape([-1 if axis == axis_at else 1 for axis in range(len(shape))])
    return factor_of


def centred(key, extent, scale, limit, cuts=(), kind=jnp.bfloat16):
    loudness = shard_levels(key, extent, cuts, -0.22, 0.18) if cuts else 1.0
    result = jax.random.normal(key, extent, jnp.float32) * scale * loudness
    return jnp.minimum(jnp.maximum(result, -limit), limit).astype(kind)


def setup_inputs(seed: int = 0) -> dict:
    splits = jax.random.split(jax.random.key(seed), 6)
    return {
        "deltas": draw_deltas(jax.random.fold_in(splits[5], 71), 0),
        "noise_first": jnp.clip(1.0 * jax.random.uniform(splits[1], (REPLICAS, PARAMS), jnp.float32) ** shard_levels(splits[1], (REPLICAS, PARAMS), ((0, 16), (1, 32)), -0.2, 0.2), 0.0, 1.0),
        "params": centred(splits[2], (PARAMS,), 1.0, 6.0, ((0, 32),), jnp.float32),
        "momentum": centred(splits[3], (PARAMS,), 1.0, 6.0, ((0, 32),), jnp.float32),
        "noise_second": jnp.clip(1.0 * jax.random.uniform(splits[4], (PARAMS,), jnp.float32) ** shard_levels(splits[4], (PARAMS,), ((0, 32),), -0.2, 0.2), 0.0, 1.0),
    }


power_list = np.array([2.0 ** k for k in range(-40, 12)], dtype=np.float32)
target_rms = 0.2
outer_rate = 0.7
outer_mu = 0.9

def quantize(values, jitter):
    initial = values.shape
    blocks = values.reshape(-1, BLOCK)
    shaken = jitter.reshape(-1, BLOCK).astype(values.dtype)
    largest = lax.optimization_barrier(jnp.max(jnp.abs(blocks), axis=1, keepdims=True))
    powers = jnp.asarray(power_list, values.dtype)[None, :]
    ceiling = lax.optimization_barrier(jnp.max(jnp.where(powers < largest, 2.0 * powers, powers[:, :1]), axis=1, keepdims=True))
    scaled = blocks * (LEVELS / ceiling)
    lower = jnp.floor(scaled)
    bumped = jnp.where(scaled - lower > shaken, 1.0, 0.0).astype(values.dtype)
    return ((lower + bumped) * (ceiling / LEVELS)).reshape(initial)

def apply_update(outer_grad, params, momentum, mean_square):
    factor = target_rms / jnp.sqrt(mean_square + 1e-06)
    update = factor * outer_grad
    new_moment = outer_mu * momentum + update
    new_param = params - outer_rate * (update + outer_mu * new_moment)
    return (new_param, new_moment)

def reference(deltas, noise_first, params, momentum, noise_second):

    def accumulate(running, pair):
        return (running + quantize(pair[0], pair[1]), None)
    summed, ignored = lax.scan(accumulate, jnp.zeros((deltas.shape[1],), deltas.dtype), (deltas, noise_first))
    average = summed / REPLICAS
    outer_grad = quantize(average, noise_second)
    return apply_update(outer_grad, params, momentum, jnp.mean(outer_grad * outer_grad))
```

```python
import functools

import jax
import jax.numpy as jnp
from jax import lax
from jax.experimental import pallas as pl
from jax.experimental.pallas import tpu as pltpu
from jax.sharding import PartitionSpec as P

BLOCK = 32
LEVELS = 8
LANES = 128
SMALLEST = 2.0**-40
F32, BF16 = jnp.float32, jnp.bfloat16

SETTINGS = pltpu.CompilerParams(vmem_limit_bytes=8 * 1024 * 1024)

target_rms = 0.2
outer_rate = 0.7
outer_mu = 0.9


def block_largest(values):
    largest = jnp.abs(values)
    lane = lax.broadcasted_iota(jnp.int32, values.shape, 1)
    step = 1
    while step < BLOCK:
        below = pltpu.roll(largest, step, 1)
        above = pltpu.roll(largest, LANES - step, 1)
        largest = jnp.maximum(largest, jnp.where((lane & step) != 0, below, above))
        step *= 2
    return largest


def power_above(largest):
    largest = jnp.maximum(largest, SMALLEST)
    ceiling = jnp.full_like(largest, SMALLEST)
    for jump in (32, 16, 8, 4, 2, 1):
        ceiling = jnp.where(ceiling * 2.0 ** (jump - 1) < largest, ceiling * 2.0**jump, ceiling)
    return ceiling


def quantized(values, jitter):
    ceiling = power_above(block_largest(values))
    scaled = values * (LEVELS / ceiling)
    lower = jnp.floor(scaled)
    bumped = jnp.where(scaled - lower > jitter, lower + 1.0, lower)
    return bumped * (ceiling * (1.0 / LEVELS))


def first_kernel(values_ref, jitter_ref, out_ref):
    out_ref[...] = quantized(values_ref[...], jitter_ref[...]).astype(BF16)


def second_kernel(count, terms_ref, jitter_ref, out_ref):
    total = terms_ref[0].astype(F32)
    for r in range(1, count):
        total = total + terms_ref[r].astype(F32)
    result = quantized(total * (1.0 / count), jitter_ref[...]).astype(BF16)
    for r in range(count):
        out_ref[r] = result


def square_kernel(grad_ref, out_ref):
    grad = grad_ref[...].astype(F32)
    partial = jnp.sum(grad * grad, axis=0, keepdims=True)
    out_ref[...] = jnp.broadcast_to(partial, out_ref.shape)


def update_kernel(full_count, squares_ref, grad_ref, params_ref, momentum_ref, new_params_ref, new_momentum_ref):
    squares = jnp.sum(squares_ref[...], keepdims=True)
    factor = target_rms / jnp.sqrt(squares * (1.0 / full_count) + 1e-06)
    update = factor * grad_ref[...].astype(F32)
    moment = outer_mu * momentum_ref[...] + update
    new_momentum_ref[...] = moment
    new_params_ref[...] = params_ref[...] - outer_rate * (update + outer_mu * moment)


def local(deltas, noise_first, params, momentum, noise_second):
    length = params.shape[0]
    rows = length // LANES
    reps, shards = lax.axis_size("rep"), lax.axis_size("fsdp")
    own = rows // reps
    steps = 4
    part = rows // steps
    block = pl.BlockSpec((part, LANES), lambda i: (i, 0))

    terms = pl.pallas_call(
        first_kernel,
        grid=(steps,),
        in_specs=[block, block],
        out_specs=block,
        out_shape=jax.ShapeDtypeStruct((rows, LANES), BF16),
        name="quantize_first",
    )(deltas.reshape(rows, LANES), noise_first.reshape(rows, LANES))

    place = lax.axis_index("rep") * own
    jitter = lax.dynamic_slice_in_dim(noise_second.reshape(rows, LANES), place, own, 0)

    met = lax.all_to_all(terms.reshape(reps, own, LANES), "rep", 0, 0, tiled=True)
    copies = pl.pallas_call(
        functools.partial(second_kernel, reps),
        out_shape=jax.ShapeDtypeStruct((reps, own, LANES), BF16),
        compiler_params=SETTINGS,
        name="sum_quantize_second",
    )(met, jitter)
    grad = lax.all_to_all(copies, "rep", 0, 0, tiled=True).reshape(rows, LANES)

    squares = pl.pallas_call(
        square_kernel,
        out_shape=jax.ShapeDtypeStruct((shards, LANES), F32),
        compiler_params=SETTINGS,
        name="squares",
    )(grad)
    squares = lax.all_to_all(squares.reshape(shards, 1, LANES), "fsdp", 0, 0, tiled=True)

    new_params, new_momentum = pl.pallas_call(
        functools.partial(update_kernel, length * shards),
        grid=(steps,),
        in_specs=[pl.BlockSpec((shards, LANES), lambda i: (0, 0)), block, block, block],
        out_specs=[block, block],
        out_shape=[jax.ShapeDtypeStruct((rows, LANES), F32)] * 2,
        compiler_params=SETTINGS,
        name="update",
    )(squares.reshape(shards, LANES), grad, params.reshape(rows, LANES), momentum.reshape(rows, LANES))
    return new_params.reshape(length), new_momentum.reshape(length)


def solution(mesh):
    in_specs = (P("rep", "fsdp"), P("rep", "fsdp"), P("fsdp"), P("fsdp"), P("fsdp"))
    out_specs = (P("fsdp"), P("fsdp"))
    return jax.shard_map(local, mesh=mesh, in_specs=in_specs, out_specs=out_specs, check_vma=False)
```

```python
import functools

import jax
import jax.numpy as jnp
from jax import lax
from jax.experimental import pallas as pl
from jax.experimental.pallas import tpu as pltpu
from jax.sharding import PartitionSpec as P

BLOCK = 32
LEVELS = 8
LANES = 128
SMALLEST = 2.0**-40
F32, BF16 = jnp.float32, jnp.bfloat16

SETTINGS = pltpu.CompilerParams(vmem_limit_bytes=8 * 1024 * 1024)

target_rms = 0.2
outer_rate = 0.7
outer_mu = 0.9


def spread_matrix():
    source = lax.broadcasted_iota(jnp.int32, (LANES, LANES), 0)
    target = lax.broadcasted_iota(jnp.int32, (LANES, LANES), 1)
    return jnp.where(source == (target | (BLOCK - 1)), 1.0, 0.0).astype(BF16)


def quantized(values, jitter):
    largest = jnp.abs(values)
    step = 1
    while step < BLOCK:
        largest = jnp.maximum(largest, pltpu.roll(largest, step, 1))
        step *= 2
    largest = jnp.maximum(largest, SMALLEST)
    widened = largest * (2.0**23 + 1.0)
    below = widened - widened * (1.0 - 2.0**-24)
    ceiling = jnp.where(below < largest, 2.0 * below, below)
    inverse = pl.reciprocal(ceiling, approx=True)
    spread = spread_matrix()
    ceiling = jnp.dot(ceiling.astype(BF16), spread, preferred_element_type=F32)
    inverse = jnp.dot(inverse.astype(BF16), spread, preferred_element_type=F32)
    scaled = values * (inverse * LEVELS)
    lower = jnp.floor(scaled)
    bumped = jnp.where(scaled - lower > jitter, lower + 1.0, lower)
    return (bumped * (ceiling * (1.0 / LEVELS))).astype(BF16)


def first_kernel(own, values_hbm, jitter_hbm, second_hbm, out_ref, second_ref, values, jitter, done):
    place = pl.multiple_of(lax.axis_index("rep") * own, own)
    copies = [
        pltpu.make_async_copy(values_hbm, values, done.at[0]),
        pltpu.make_async_copy(jitter_hbm, jitter, done.at[1]),
        pltpu.make_async_copy(second_hbm.at[pl.ds(place, own)], second_ref, done.at[2]),
    ]
    for copy in copies:
        copy.start()
    for copy in copies:
        copy.wait()
    out_ref[...] = quantized(values[...], jitter[...])


def second_kernel(count, terms_ref, jitter_ref, out_ref):
    total = terms_ref[0].astype(F32)
    for r in range(1, count):
        total = total + terms_ref[r].astype(F32)
    result = quantized(total * (1.0 / count), jitter_ref[...])
    for r in range(count):
        out_ref[r] = result


def square_kernel(grad_ref, out_ref):
    grad = grad_ref[...].astype(F32)
    partial = jnp.sum(grad * grad, axis=0, keepdims=True)
    out_ref[...] = jnp.broadcast_to(partial, out_ref.shape)


def update_kernel(full_count, chunks, squares_ref, grad_ref, params_ref, momentum_ref, new_params_hbm, new_momentum_hbm, new_params, new_momentum, done):
    squares = jnp.sum(squares_ref[...], keepdims=True)
    factor = target_rms / jnp.sqrt(squares * (1.0 / full_count) + 1e-06)
    rows = grad_ref.shape[0] // chunks
    copies = []
    for i in range(chunks):
        part = pl.ds(i * rows, rows)
        update = factor * grad_ref[part].astype(F32)
        moment = outer_mu * momentum_ref[part] + update
        new_momentum[part] = moment
        new_params[part] = params_ref[part] - outer_rate * (update + outer_mu * moment)
        copies += [
            pltpu.make_async_copy(new_momentum.at[part], new_momentum_hbm.at[part], done.at[0, i]),
            pltpu.make_async_copy(new_params.at[part], new_params_hbm.at[part], done.at[1, i]),
        ]
        copies[-2].start()
        copies[-1].start()
    for copy in copies:
        copy.wait()


def local(deltas, noise_first, params, momentum, noise_second):
    length = params.shape[0]
    rows = length // LANES
    reps, shards = lax.axis_size("rep"), lax.axis_size("fsdp")
    own = rows // reps
    chunks = 4
    in_hbm = [
        pltpu.with_memory_space_constraint(array.reshape(rows, LANES), pltpu.HBM)
        for array in (deltas, noise_first, noise_second)
    ]
    terms, jitter = pl.pallas_call(
        functools.partial(first_kernel, own),
        in_specs=[pl.BlockSpec(memory_space=pltpu.HBM)] * 3,
        out_specs=[pl.BlockSpec(memory_space=pltpu.VMEM)] * 2,
        out_shape=[jax.ShapeDtypeStruct((rows, LANES), BF16), jax.ShapeDtypeStruct((own, LANES), F32)],
        scratch_shapes=[pltpu.VMEM((rows, LANES), F32)] * 2 + [pltpu.SemaphoreType.DMA((3,))],
        compiler_params=SETTINGS,
        name="quantize_first",
    )(*in_hbm)

    met = lax.all_to_all(terms.reshape(reps, own, LANES), "rep", 0, 0, tiled=True)
    copies = pl.pallas_call(
        functools.partial(second_kernel, reps),
        out_shape=jax.ShapeDtypeStruct((reps, own, LANES), BF16),
        compiler_params=SETTINGS,
        name="sum_quantize_second",
    )(met, jitter)
    grad = lax.all_to_all(copies, "rep", 0, 0, tiled=True).reshape(rows, LANES)

    squares = pl.pallas_call(
        square_kernel,
        out_shape=jax.ShapeDtypeStruct((shards, LANES), F32),
        compiler_params=SETTINGS,
        name="squares",
    )(grad)
    squares = lax.all_to_all(squares.reshape(shards, 1, LANES), "fsdp", 0, 0, tiled=True)

    new_params, new_momentum = pl.pallas_call(
        functools.partial(update_kernel, length * shards, chunks),
        in_specs=[pl.BlockSpec(memory_space=pltpu.VMEM)] * 4,
        out_specs=[pl.BlockSpec(memory_space=pltpu.HBM)] * 2,
        out_shape=[jax.ShapeDtypeStruct((rows, LANES), F32)] * 2,
        scratch_shapes=[pltpu.VMEM((rows, LANES), F32)] * 2 + [pltpu.SemaphoreType.DMA((2, chunks))],
        compiler_params=SETTINGS,
        name="update",
    )(squares.reshape(shards, LANES), grad, params.reshape(rows, LANES), momentum.reshape(rows, LANES))
    return new_params.reshape(length), new_momentum.reshape(length)


def solution(mesh):
    in_specs = (P("rep", "fsdp"), P("rep", "fsdp"), P("fsdp"), P("fsdp"), P("fsdp"))
    out_specs = (P("fsdp"), P("fsdp"))
    return jax.shard_map(local, mesh=mesh, in_specs=in_specs, out_specs=out_specs, check_vma=False)
```

```python
import functools

import jax
import jax.numpy as jnp
from jax import lax
from jax.experimental import pallas as pl
from jax.experimental.pallas import tpu as pltpu
from jax.sharding import PartitionSpec as P

BLOCK = 32
LEVELS = 8
LANES = 128
SMALLEST = 2.0**-40
F32, BF16 = jnp.float32, jnp.bfloat16

SETTINGS = pltpu.CompilerParams(vmem_limit_bytes=8 * 1024 * 1024)

TAIL = 16
HALVES, SCALARS_FIRST = True, False
target_rms = 0.2
outer_rate = 0.7
outer_mu = 0.9


def spread_matrix():
    source = lax.broadcasted_iota(jnp.int32, (LANES, LANES), 0)
    target = lax.broadcasted_iota(jnp.int32, (LANES, LANES), 1)
    return jnp.where(source == (target | (BLOCK - 1)), 1.0, 0.0).astype(BF16)


def quantized(values, jitter):
    largest = jnp.abs(values)
    step = 1
    while step < BLOCK:
        largest = jnp.maximum(largest, pltpu.roll(largest, step, 1))
        step *= 2
    largest = jnp.maximum(largest, SMALLEST)
    widened = largest * (2.0**23 + 1.0)
    below = widened - widened * (1.0 - 2.0**-24)
    ceiling = jnp.where(below < largest, 2.0 * below, below)
    inverse = pl.reciprocal(ceiling, approx=True)
    spread = spread_matrix()
    ceiling = jnp.dot(ceiling.astype(BF16), spread, preferred_element_type=F32)
    inverse = jnp.dot(inverse.astype(BF16), spread, preferred_element_type=F32)
    scaled = values * (inverse * LEVELS)
    lower = jnp.floor(scaled)
    bumped = jnp.where(scaled - lower > jitter, lower + 1.0, lower)
    return (bumped * (ceiling * (1.0 / LEVELS))).astype(BF16)


def first_kernel(own, group, values_hbm, jitter_hbm, second_hbm, out_ref, second_ref, values, jitter, done):
    place = pl.multiple_of(lax.rem(lax.axis_index("rep"), group) * own, own)
    copies = [
        pltpu.make_async_copy(values_hbm, values, done.at[0]),
        pltpu.make_async_copy(jitter_hbm, jitter, done.at[1]),
        pltpu.make_async_copy(second_hbm.at[pl.ds(place, own)], second_ref, done.at[2]),
    ]
    for copy in copies:
        copy.start()
    for copy in copies:
        copy.wait()
    out_ref[...] = quantized(values[...], jitter[...])


def added(terms_ref):
    total = terms_ref[0].astype(F32)
    for r in range(1, terms_ref.shape[0]):
        total = total + terms_ref[r].astype(F32)
    return total


def partial_kernel(terms_ref, out_ref):
    out_ref[...] = added(terms_ref)


def square_message(grad, out_ref):
    grad = grad.astype(F32)
    out_ref[...] = jnp.broadcast_to(jnp.sum(grad * grad, axis=0, keepdims=True), out_ref.shape)


def second_kernel(reps, terms_ref, jitter_ref, out_ref, message_ref):
    grad = quantized(added(terms_ref) * (1.0 / reps), jitter_ref[...])
    out_ref[...] = grad
    square_message(grad, message_ref)


def second_copies_kernel(reps, terms_ref, jitter_ref, out_ref):
    grad = quantized(added(terms_ref) * (1.0 / reps), jitter_ref[...])
    for r in range(out_ref.shape[0]):
        out_ref[r] = grad


def second_halves_kernel(reps, near_ref, far_ref, jitter_ref, out_ref, message_ref):
    grad = quantized((near_ref[...] + far_ref[...]) * (1.0 / reps), jitter_ref[...])
    out_ref[...] = grad
    square_message(grad, message_ref)


def second_halves_copies_kernel(reps, near_ref, far_ref, jitter_ref, out_ref):
    grad = quantized((near_ref[...] + far_ref[...]) * (1.0 / reps), jitter_ref[...])
    for r in range(out_ref.shape[0]):
        out_ref[r] = grad


def square_kernel(grad_ref, out_ref):
    square_message(grad_ref[...], out_ref)


def join_kernel(grad_ref, squares_ref, out_ref):
    own = grad_ref.shape[0]
    squares = jnp.sum(squares_ref[...], axis=0, keepdims=True)
    high = squares.astype(BF16).astype(F32)
    middle = (squares - high).astype(BF16).astype(F32)
    low = squares - high - middle
    row = lax.broadcasted_iota(jnp.int32, (TAIL, LANES), 0)
    tail = jnp.where(row == 0, high, jnp.where(row == 1, middle, jnp.where(row == 2, low, 0.0))).astype(BF16)
    grad = grad_ref[...]
    for r in range(out_ref.shape[0]):
        out_ref[r, 0:own] = grad
        out_ref[r, own : own + TAIL] = tail


def update_kernel(full_count, chunks, squares_ref, grad_ref, params_ref, momentum_ref, new_params_hbm, new_momentum_hbm, new_params, new_momentum, done):
    joined = squares_ref is None
    if joined:
        count, own = grad_ref.shape[0], grad_ref.shape[1] - TAIL
        squares = jnp.sum(grad_ref[:, own : own + TAIL].astype(F32), keepdims=True).reshape(1, 1)
        rows = count * own // chunks
    else:
        squares = jnp.sum(squares_ref[...], keepdims=True)
        rows = grad_ref.shape[0] // chunks
    factor = target_rms / jnp.sqrt(squares * (1.0 / full_count) + 1e-06)
    copies = []
    for i in range(chunks):
        part = pl.ds(i * rows, rows)
        if joined:
            some = count // chunks
            grad = grad_ref[i * some : (i + 1) * some, 0:own].astype(F32).reshape(rows, LANES)
        else:
            grad = grad_ref[part].astype(F32)
        update = factor * grad
        moment = outer_mu * momentum_ref[part] + update
        new_momentum[part] = moment
        new_params[part] = params_ref[part] - outer_rate * (update + outer_mu * moment)
        copies += [
            pltpu.make_async_copy(new_momentum.at[part], new_momentum_hbm.at[part], done.at[0, i]),
            pltpu.make_async_copy(new_params.at[part], new_params_hbm.at[part], done.at[1, i]),
        ]
        copies[-2].start()
        copies[-1].start()
    for copy in copies:
        copy.wait()


def call(kernel, shapes, name, *arrays):
    out = [jax.ShapeDtypeStruct(shape, kind) for shape, kind in shapes]
    return pl.pallas_call(kernel, out_shape=out, compiler_params=SETTINGS, name=name)(*arrays)


def local(deltas, noise_first, params, momentum, noise_second):
    length = params.shape[0]
    rows = length // LANES
    reps, shards = lax.axis_size("rep"), lax.axis_size("fsdp")
    near = reps // 2
    group = near if HALVES else reps
    own = rows // group
    chunks = 4
    sides = [list(range(near)), list(range(near, reps))] if HALVES else None

    def exchanged(array):
        return lax.all_to_all(array, "rep", 0, 0, axis_index_groups=sides, tiled=True)

    in_hbm = [
        pltpu.with_memory_space_constraint(array.reshape(rows, LANES), pltpu.HBM)
        for array in (deltas, noise_first, noise_second)
    ]
    terms, jitter = pl.pallas_call(
        functools.partial(first_kernel, own, group),
        in_specs=[pl.BlockSpec(memory_space=pltpu.HBM)] * 3,
        out_specs=[pl.BlockSpec(memory_space=pltpu.VMEM)] * 2,
        out_shape=[jax.ShapeDtypeStruct((rows, LANES), BF16), jax.ShapeDtypeStruct((own, LANES), F32)],
        scratch_shapes=[pltpu.VMEM((rows, LANES), F32)] * 2 + [pltpu.SemaphoreType.DMA((3,))],
        compiler_params=SETTINGS,
        name="quantize_first",
    )(*in_hbm)
    met = exchanged(terms.reshape(group, own, LANES))
    copied, message = ((group, own, LANES), BF16), ((shards, LANES), F32)
    if HALVES:
        (partial,) = call(partial_kernel, [((own, LANES), F32)], "partial", met)
        other = lax.ppermute(partial, "rep", [(r, (r + near) % reps) for r in range(reps)])
        sums = (partial, other)
        kernels = (second_halves_kernel, second_halves_copies_kernel)
    else:
        sums = (met,)
        kernels = (second_kernel, second_copies_kernel)
    if SCALARS_FIRST:
        grad, squares = call(functools.partial(kernels[0], reps), [((own, LANES), BF16), message], "second", *sums, jitter)
        squares = lax.all_to_all(squares.reshape(shards, 1, LANES), "fsdp", 0, 0, tiled=True).reshape(shards, LANES)
        (copies,) = call(join_kernel, [((group, own + TAIL, LANES), BF16)], "join", grad, squares)
        last = (exchanged(copies),)
        update = functools.partial(update_kernel, length * shards, chunks, None)
    else:
        (copies,) = call(functools.partial(kernels[1], reps), [copied], "second", *sums, jitter)
        grad = exchanged(copies).reshape(rows, LANES)
        (squares,) = call(square_kernel, [message], "squares", grad)
        squares = lax.all_to_all(squares.reshape(shards, 1, LANES), "fsdp", 0, 0, tiled=True)
        last = (squares.reshape(shards, LANES), grad)
        update = functools.partial(update_kernel, length * shards, chunks)

    new_params, new_momentum = pl.pallas_call(
        update,
        in_specs=[pl.BlockSpec(memory_space=pltpu.VMEM)] * (len(last) + 2),
        out_specs=[pl.BlockSpec(memory_space=pltpu.HBM)] * 2,
        out_shape=[jax.ShapeDtypeStruct((rows, LANES), F32)] * 2,
        scratch_shapes=[pltpu.VMEM((rows, LANES), F32)] * 2 + [pltpu.SemaphoreType.DMA((2, chunks))],
        compiler_params=SETTINGS,
        name="update",
    )(*last, params.reshape(rows, LANES), momentum.reshape(rows, LANES))
    return new_params.reshape(length), new_momentum.reshape(length)


def solution(mesh):
    in_specs = (P("rep", "fsdp"), P("rep", "fsdp"), P("fsdp"), P("fsdp"), P("fsdp"))
    out_specs = (P("fsdp"), P("fsdp"))
    return jax.shard_map(local, mesh=mesh, in_specs=in_specs, out_specs=out_specs, check_vma=False)
```

```python
import functools

import jax
import jax.numpy as jnp
from jax import lax
from jax.experimental import pallas as pl
from jax.experimental.pallas import tpu as pltpu
from jax.sharding import PartitionSpec as P

BLOCK = 32
LEVELS = 8
LANES = 128
SMALLEST = 2.0**-40
F32, BF16 = jnp.float32, jnp.bfloat16

SETTINGS = pltpu.CompilerParams(vmem_limit_bytes=8 * 1024 * 1024)

target_rms = 0.2
outer_rate = 0.7
outer_mu = 0.9


def spread_matrix(value):
    source = lax.broadcasted_iota(jnp.int32, (LANES, LANES), 0)
    target = lax.broadcasted_iota(jnp.int32, (LANES, LANES), 1)
    return jnp.where(source == (target | (BLOCK - 1)), value, 0.0).astype(BF16)


def quantized(values, jitter, strides):
    size = jnp.maximum(jnp.abs(values), SMALLEST) * (2.0 - 2.0**-23)
    widened = size * (2.0**23 + 1.0)
    ceiling = (widened - widened * (1.0 - 2.0**-24)).astype(BF16)
    step = 1
    for stride in strides:
        rolled = [pltpu.roll(ceiling, step * i, 1) for i in range(1, stride)]
        ceiling = functools.reduce(jnp.maximum, rolled, ceiling)
        step *= stride
    inverse = pl.reciprocal(ceiling.astype(F32), approx=True).astype(BF16)
    quantum = jnp.dot(ceiling, spread_matrix(1.0 / LEVELS), preferred_element_type=F32)
    inverse = jnp.dot(inverse, spread_matrix(1.0 * LEVELS), preferred_element_type=F32)
    scaled = values * inverse
    lower = jnp.floor(scaled)
    bumped = jnp.where(scaled - lower > jitter, lower + 1.0, lower)
    return (bumped * quantum).astype(BF16)


def first_kernel(own, group, values_hbm, jitter_hbm, second_hbm, out_ref, second_ref, values, jitter, done):
    place = pl.multiple_of(lax.rem(lax.axis_index("rep"), group) * own, own)
    copies = [
        pltpu.make_async_copy(values_hbm, values, done.at[0]),
        pltpu.make_async_copy(jitter_hbm, jitter, done.at[1]),
        pltpu.make_async_copy(second_hbm.at[pl.ds(place, own)], second_ref, done.at[2]),
    ]
    for copy in copies:
        copy.start()
    for copy in copies:
        copy.wait()
    out_ref[...] = quantized(values[...], jitter[...], (2, 2, 2, 2, 2))


def partial_kernel(terms_ref, out_ref):
    total = terms_ref[0].astype(F32)
    for r in range(1, terms_ref.shape[0]):
        total = total + terms_ref[r].astype(F32)
    out_ref[...] = total


def second_kernel(reps, near_ref, far_ref, jitter_ref, out_ref):
    average = (near_ref[...] + far_ref[...]) * (1.0 / reps)
    grad = quantized(average, jitter_ref[...], (4, 8))
    for r in range(out_ref.shape[0]):
        out_ref[r] = grad


def square_kernel(grad_ref, out_ref):
    grad = grad_ref[...].astype(F32)
    out_ref[...] = jnp.broadcast_to(jnp.sum(grad * grad, axis=0, keepdims=True), out_ref.shape)


def update_kernel(full_count, chunks, squares_ref, grad_ref, params_ref, momentum_ref, new_params_hbm, new_momentum_hbm, new_params, new_momentum, done):
    squares = jnp.sum(squares_ref[...], keepdims=True)
    factor = target_rms * lax.rsqrt(squares * (1.0 / full_count) + 1e-06)
    rows = grad_ref.shape[0] // chunks
    copies = []
    for i in range(chunks):
        part = pl.ds(i * rows, rows)
        update = factor * grad_ref[part].astype(F32)
        moment = outer_mu * momentum_ref[part] + update
        new_momentum[part] = moment
        new_params[part] = params_ref[part] - outer_rate * (update + outer_mu * moment)
        copies += [
            pltpu.make_async_copy(new_momentum.at[part], new_momentum_hbm.at[part], done.at[0, i]),
            pltpu.make_async_copy(new_params.at[part], new_params_hbm.at[part], done.at[1, i]),
        ]
        copies[-2].start()
        copies[-1].start()
    for copy in copies:
        copy.wait()


def call(kernel, shape, kind, name, *arrays):
    out = jax.ShapeDtypeStruct(shape, kind)
    return pl.pallas_call(kernel, out_shape=out, compiler_params=SETTINGS, name=name)(*arrays)


def local(deltas, noise_first, params, momentum, noise_second):
    length = params.shape[0]
    rows = length // LANES
    reps, shards = lax.axis_size("rep"), lax.axis_size("fsdp")
    near = reps // 2
    own = rows // near
    chunks = 4
    halves = [list(range(near)), list(range(near, reps))]

    def exchanged(array):
        return lax.all_to_all(array, "rep", 0, 0, axis_index_groups=halves, tiled=True)

    in_hbm = [
        pltpu.with_memory_space_constraint(array.reshape(rows, LANES), pltpu.HBM)
        for array in (deltas, noise_first, noise_second)
    ]
    terms, jitter = pl.pallas_call(
        functools.partial(first_kernel, own, near),
        in_specs=[pl.BlockSpec(memory_space=pltpu.HBM)] * 3,
        out_specs=[pl.BlockSpec(memory_space=pltpu.VMEM)] * 2,
        out_shape=[jax.ShapeDtypeStruct((rows, LANES), BF16), jax.ShapeDtypeStruct((own, LANES), F32)],
        scratch_shapes=[pltpu.VMEM((rows, LANES), F32)] * 2 + [pltpu.SemaphoreType.DMA((3,))],
        compiler_params=SETTINGS,
        name="quantize_first",
    )(*in_hbm)
    met = exchanged(terms.reshape(near, own, LANES))
    partial = call(partial_kernel, (own, LANES), F32, "partial", met)
    other = lax.ppermute(partial, "rep", [(r, (r + near) % reps) for r in range(reps)])
    second = functools.partial(second_kernel, reps)
    copies = call(second, (near, own, LANES), BF16, "quantize_second", partial, other, jitter)
    grad = exchanged(copies).reshape(rows, LANES)
    squares = call(square_kernel, (shards, LANES), F32, "squares", grad)
    squares = lax.all_to_all(squares.reshape(shards, 1, LANES), "fsdp", 0, 0, tiled=True)

    new_params, new_momentum = pl.pallas_call(
        functools.partial(update_kernel, length * shards, chunks),
        in_specs=[pl.BlockSpec(memory_space=pltpu.VMEM)] * 4,
        out_specs=[pl.BlockSpec(memory_space=pltpu.HBM)] * 2,
        out_shape=[jax.ShapeDtypeStruct((rows, LANES), F32)] * 2,
        scratch_shapes=[pltpu.VMEM((rows, LANES), F32)] * 2 + [pltpu.SemaphoreType.DMA((2, chunks))],
        compiler_params=SETTINGS,
        name="update",
    )(squares.reshape(shards, LANES), grad, params.reshape(rows, LANES), momentum.reshape(rows, LANES))
    return new_params.reshape(length), new_momentum.reshape(length)


def solution(mesh):
    in_specs = (P("rep", "fsdp"), P("rep", "fsdp"), P("fsdp"), P("fsdp"), P("fsdp"))
    out_specs = (P("fsdp"), P("fsdp"))
    return jax.shard_map(local, mesh=mesh, in_specs=in_specs, out_specs=out_specs, check_vma=False)
```

```python
import functools

import jax
import jax.numpy as jnp
from jax import lax
from jax.experimental import pallas as pl
from jax.experimental.pallas import tpu as pltpu
from jax.sharding import PartitionSpec as P

BLOCK = 32
LEVELS = 8
LANES = 128
SMALLEST = 2.0**-40
F32, BF16 = jnp.float32, jnp.bfloat16

SETTINGS = pltpu.CompilerParams(vmem_limit_bytes=8 * 1024 * 1024)

target_rms = 0.2
outer_rate = 0.7
outer_mu = 0.9


def spread_matrix(value):
    source = lax.broadcasted_iota(jnp.int32, (LANES, LANES), 0)
    target = lax.broadcasted_iota(jnp.int32, (LANES, LANES), 1)
    return jnp.where(source == (target | (BLOCK - 1)), value, 0.0).astype(BF16)


def quantized(values, jitter, strides):
    size = jnp.maximum(jnp.abs(values), SMALLEST) * (2.0 - 2.0**-23)
    widened = size * (2.0**23 + 1.0)
    ceiling = (widened - widened * (1.0 - 2.0**-24)).astype(BF16)
    step = 1
    for stride in strides:
        rolled = [pltpu.roll(ceiling, step * i, 1) for i in range(1, stride)]
        ceiling = functools.reduce(jnp.maximum, rolled, ceiling)
        step *= stride
    inverse = pl.reciprocal(ceiling.astype(F32), approx=True).astype(BF16)
    quantum = jnp.dot(ceiling, spread_matrix(1.0 / LEVELS), preferred_element_type=F32)
    inverse = jnp.dot(inverse, spread_matrix(1.0 * LEVELS), preferred_element_type=F32)
    scaled = values * inverse
    lower = jnp.floor(scaled)
    bumped = jnp.where(scaled - lower > jitter, lower + 1.0, lower)
    return (bumped * quantum).astype(BF16)


def first_kernel(own, group, values_hbm, jitter_hbm, second_hbm, out_ref, second_ref, values, jitter, done):
    place = pl.multiple_of(lax.rem(lax.axis_index("rep") + 3, group) * own, own)
    copies = [
        pltpu.make_async_copy(values_hbm, values, done.at[0]),
        pltpu.make_async_copy(jitter_hbm, jitter, done.at[1]),
        pltpu.make_async_copy(second_hbm.at[pl.ds(place, own)], second_ref, done.at[2]),
    ]
    for copy in copies:
        copy.start()
    for copy in copies:
        copy.wait()
    out_ref[...] = quantized(values[...], jitter[...], (2, 2, 2, 2, 2))


def partial_kernel(terms_ref, out_ref):
    total = terms_ref[0].astype(F32)
    for r in range(1, terms_ref.shape[0]):
        total = total + terms_ref[r].astype(F32)
    out_ref[...] = total


def second_kernel(reps, near_ref, far_ref, jitter_ref, out_ref):
    average = (near_ref[...] + far_ref[...]) * (1.0 / reps)
    grad = quantized(average, jitter_ref[...], (4, 8))
    for r in range(out_ref.shape[0]):
        out_ref[r] = grad


def square_kernel(grad_ref, out_ref):
    grad = grad_ref[...].astype(F32)
    out_ref[...] = jnp.broadcast_to(jnp.sum(grad * grad, axis=0, keepdims=True), out_ref.shape)


def update_kernel(full_count, chunks, squares_ref, grad_ref, params_ref, momentum_ref, new_params_hbm, new_momentum_hbm, new_params, new_momentum, done):
    squares = jnp.sum(squares_ref[...], keepdims=True)
    factor = target_rms * lax.rsqrt(squares * (1.0 / full_count) + 1e-06)
    rows = grad_ref.shape[0] // chunks
    copies = []
    for i in range(chunks):
        part = pl.ds(i * rows, rows)
        update = factor * grad_ref[part].astype(F32)
        moment = outer_mu * momentum_ref[part] + update
        new_momentum[part] = moment
        new_params[part] = params_ref[part] - outer_rate * (update + outer_mu * moment)
        copies += [
            pltpu.make_async_copy(new_momentum.at[part], new_momentum_hbm.at[part], done.at[0, i]),
            pltpu.make_async_copy(new_params.at[part], new_params_hbm.at[part], done.at[1, i]),
        ]
        copies[-2].start()
        copies[-1].start()
    for copy in copies:
        copy.wait()


def call(kernel, shape, kind, name, *arrays):
    out = jax.ShapeDtypeStruct(shape, kind)
    return pl.pallas_call(kernel, out_shape=out, compiler_params=SETTINGS, name=name)(*arrays)


def local(deltas, noise_first, params, momentum, noise_second):
    length = params.shape[0]
    rows = length // LANES
    reps, shards = lax.axis_size("rep"), lax.axis_size("fsdp")
    near = reps // 2
    own = rows // near
    chunks = 4
    halves = [[k for k in [5, 6, 7, 0, 1, 2, 3, 4]], [near + k for k in [5, 6, 7, 0, 1, 2, 3, 4]]]

    def exchanged(array):
        return lax.all_to_all(array, "rep", 0, 0, axis_index_groups=halves, tiled=True)

    in_hbm = [
        pltpu.with_memory_space_constraint(array.reshape(rows, LANES), pltpu.HBM)
        for array in (deltas, noise_first, noise_second)
    ]
    terms, jitter = pl.pallas_call(
        functools.partial(first_kernel, own, near),
        in_specs=[pl.BlockSpec(memory_space=pltpu.HBM)] * 3,
        out_specs=[pl.BlockSpec(memory_space=pltpu.VMEM)] * 2,
        out_shape=[jax.ShapeDtypeStruct((rows, LANES), BF16), jax.ShapeDtypeStruct((own, LANES), F32)],
        scratch_shapes=[pltpu.VMEM((rows, LANES), F32)] * 2 + [pltpu.SemaphoreType.DMA((3,))],
        compiler_params=SETTINGS,
        name="quantize_first",
    )(*in_hbm)
    met = exchanged(terms.reshape(near, own, LANES))
    partial = call(partial_kernel, (own, LANES), F32, "partial", met)
    other = lax.ppermute(partial, "rep", [(r, (r + near) % reps) for r in range(reps)])
    second = functools.partial(second_kernel, reps)
    copies = call(second, (near, own, LANES), BF16, "quantize_second", partial, other, jitter)
    grad = exchanged(copies).reshape(rows, LANES)
    squares = call(square_kernel, (shards, LANES), F32, "squares", grad)
    squares = lax.all_to_all(squares.reshape(shards, 1, LANES), "fsdp", 0, 0, axis_index_groups=[[29, 0, 1, 2, 3, 4, 5, 6, 7, 8, 9, 10, 11, 12, 13, 14, 15, 16, 17, 18, 19, 20, 21, 22, 23, 24, 25, 26, 27, 28, 30, 31]], tiled=True)

    new_params, new_momentum = pl.pallas_call(
        functools.partial(update_kernel, length * shards, chunks),
        in_specs=[pl.BlockSpec(memory_space=pltpu.VMEM)] * 4,
        out_specs=[pl.BlockSpec(memory_space=pltpu.HBM)] * 2,
        out_shape=[jax.ShapeDtypeStruct((rows, LANES), F32)] * 2,
        scratch_shapes=[pltpu.VMEM((rows, LANES), F32)] * 2 + [pltpu.SemaphoreType.DMA((2, chunks))],
        compiler_params=SETTINGS,
        name="update",
    )(squares.reshape(shards, LANES), grad, params.reshape(rows, LANES), momentum.reshape(rows, LANES))
    return new_params.reshape(length), new_momentum.reshape(length)


def solution(mesh):
    in_specs = (P("rep", "fsdp"), P("rep", "fsdp"), P("fsdp"), P("fsdp"), P("fsdp"))
    out_specs = (P("fsdp"), P("fsdp"))
    return jax.shard_map(local, mesh=mesh, in_specs=in_specs, out_specs=out_specs, check_vma=False)
```

```python
import functools

import jax
import jax.numpy as jnp
from jax import lax
from jax.experimental import pallas as pl
from jax.experimental.pallas import tpu as pltpu
from jax.sharding import PartitionSpec as P

BLOCK = 32
LEVELS = 8
LANES = 128
SMALLEST = 2.0**-40
F32, BF16 = jnp.float32, jnp.bfloat16

SETTINGS = pltpu.CompilerParams(vmem_limit_bytes=8 * 1024 * 1024)

FIRST = 5
RUN = 4

target_rms = 0.2
outer_rate = 0.7
outer_mu = 0.9


def spread_matrix(value):
    source = lax.broadcasted_iota(jnp.int32, (LANES, LANES), 0)
    target = lax.broadcasted_iota(jnp.int32, (LANES, LANES), 1)
    return jnp.where(source == (target | (BLOCK - 1)), value, 0.0).astype(BF16)


def quantized(values, jitter, strides):
    size = jnp.maximum(jnp.abs(values), SMALLEST) * (2.0 - 2.0**-23)
    widened = size * (2.0**23 + 1.0)
    ceiling = (widened - widened * (1.0 - 2.0**-24)).astype(BF16)
    step = 1
    for stride in strides:
        rolled = [pltpu.roll(ceiling, step * i, 1) for i in range(1, stride)]
        ceiling = functools.reduce(jnp.maximum, rolled, ceiling)
        step *= stride
    inverse = pl.reciprocal(ceiling.astype(F32), approx=True).astype(BF16)
    quantum = jnp.dot(ceiling, spread_matrix(1.0 / LEVELS), preferred_element_type=F32)
    inverse = jnp.dot(inverse, spread_matrix(1.0 * LEVELS), preferred_element_type=F32)
    scaled = values * inverse
    lower = jnp.floor(scaled)
    bumped = jnp.where(scaled - lower > jitter, lower + 1.0, lower)
    return (bumped * quantum).astype(BF16)


def first_kernel(own, group, values_hbm, jitter_hbm, second_hbm, out_ref, second_ref, values, jitter, done):
    place = pl.multiple_of(lax.rem(lax.axis_index("rep") + group - FIRST, group) * own, own)
    copies = [
        pltpu.make_async_copy(values_hbm, values, done.at[0]),
        pltpu.make_async_copy(jitter_hbm, jitter, done.at[1]),
        pltpu.make_async_copy(second_hbm.at[pl.ds(place, own)], second_ref, done.at[2]),
    ]
    for copy in copies:
        copy.start()
    for copy in copies:
        copy.wait()
    out_ref[...] = quantized(values[...], jitter[...], (2, 2, 2, 2, 2))


def partial_kernel(terms_ref, out_ref):
    total = terms_ref[0].astype(F32)
    for r in range(1, terms_ref.shape[0]):
        total = total + terms_ref[r].astype(F32)
    out_ref[...] = total


def second_kernel(reps, near_ref, far_ref, jitter_ref, out_ref):
    average = (near_ref[...] + far_ref[...]) * (1.0 / reps)
    grad = quantized(average, jitter_ref[...], (4, 8))
    for r in range(out_ref.shape[0]):
        out_ref[r] = grad


def square_kernel(grad_ref, out_ref):
    grad = grad_ref[...].astype(F32)
    out_ref[...] = jnp.broadcast_to(jnp.sum(grad * grad, axis=0, keepdims=True), out_ref.shape)


def update_kernel(full_count, chunks, squares_ref, grad_ref, params_ref, momentum_ref, new_params_hbm, new_momentum_hbm, new_params, new_momentum, done):
    squares = jnp.sum(squares_ref[...], keepdims=True)
    factor = target_rms * lax.rsqrt(squares * (1.0 / full_count) + 1e-06)
    rows = grad_ref.shape[0] // chunks
    copies = []
    for i in range(chunks):
        part = pl.ds(i * rows, rows)
        update = factor * grad_ref[part].astype(F32)
        moment = outer_mu * momentum_ref[part] + update
        new_momentum[part] = moment
        new_params[part] = params_ref[part] - outer_rate * (update + outer_mu * moment)
        copies += [
            pltpu.make_async_copy(new_momentum.at[part], new_momentum_hbm.at[part], done.at[0, i]),
            pltpu.make_async_copy(new_params.at[part], new_params_hbm.at[part], done.at[1, i]),
        ]
        copies[-2].start()
        copies[-1].start()
    for copy in copies:
        copy.wait()


def scalar_groups(reps, shards):
    groups = []
    for even in range(0, reps, 2):
        odd = even + 1
        one = shards - RUN + (RUN // 2 if even < reps // 2 else RUN // 2 - 1)
        two = one - RUN
        groups.append([odd * shards + one] + [even * shards + f for f in range(shards) if f != one])
        rest = [(even if f == one else odd) * shards + f for f in range(shards) if f != two]
        groups.append([odd * shards + two] + rest)
    return groups


def call(kernel, shape, kind, name, *arrays):
    out = jax.ShapeDtypeStruct(shape, kind)
    return pl.pallas_call(kernel, out_shape=out, compiler_params=SETTINGS, name=name)(*arrays)


def local(deltas, noise_first, params, momentum, noise_second):
    length = params.shape[0]
    rows = length // LANES
    reps, shards = lax.axis_size("rep"), lax.axis_size("fsdp")
    near = reps // 2
    own = rows // near
    chunks = 4
    turned = [(k + FIRST) % near for k in range(near)]
    halves = [turned, [near + k for k in turned]]

    def exchanged(array):
        return lax.all_to_all(array, "rep", 0, 0, axis_index_groups=halves, tiled=True)

    in_hbm = [
        pltpu.with_memory_space_constraint(array.reshape(rows, LANES), pltpu.HBM)
        for array in (deltas, noise_first, noise_second)
    ]
    terms, jitter = pl.pallas_call(
        functools.partial(first_kernel, own, near),
        in_specs=[pl.BlockSpec(memory_space=pltpu.HBM)] * 3,
        out_specs=[pl.BlockSpec(memory_space=pltpu.VMEM)] * 2,
        out_shape=[jax.ShapeDtypeStruct((rows, LANES), BF16), jax.ShapeDtypeStruct((own, LANES), F32)],
        scratch_shapes=[pltpu.VMEM((rows, LANES), F32)] * 2 + [pltpu.SemaphoreType.DMA((3,))],
        compiler_params=SETTINGS,
        name="quantize_first",
    )(*in_hbm)
    met = exchanged(terms.reshape(near, own, LANES))
    partial = call(partial_kernel, (own, LANES), F32, "partial", met)
    other = lax.ppermute(partial, "rep", [(r, (r + near) % reps) for r in range(reps)])
    second = functools.partial(second_kernel, reps)
    copies = call(second, (near, own, LANES), BF16, "quantize_second", partial, other, jitter)
    grad = exchanged(copies).reshape(rows, LANES)
    squares = call(square_kernel, (shards, LANES), F32, "squares", grad)
    groups = scalar_groups(reps, shards)
    squares = squares.reshape(shards, 1, LANES)
    squares = lax.all_to_all(squares, ("rep", "fsdp"), 0, 0, axis_index_groups=groups, tiled=True)

    new_params, new_momentum = pl.pallas_call(
        functools.partial(update_kernel, length * shards, chunks),
        in_specs=[pl.BlockSpec(memory_space=pltpu.VMEM)] * 4,
        out_specs=[pl.BlockSpec(memory_space=pltpu.HBM)] * 2,
        out_shape=[jax.ShapeDtypeStruct((rows, LANES), F32)] * 2,
        scratch_shapes=[pltpu.VMEM((rows, LANES), F32)] * 2 + [pltpu.SemaphoreType.DMA((2, chunks))],
        compiler_params=SETTINGS,
        name="update",
    )(squares.reshape(shards, LANES), grad, params.reshape(rows, LANES), momentum.reshape(rows, LANES))
    return new_params.reshape(length), new_momentum.reshape(length)


def solution(mesh):
    in_specs = (P("rep", "fsdp"), P("rep", "fsdp"), P("fsdp"), P("fsdp"), P("fsdp"))
    out_specs = (P("fsdp"), P("fsdp"))
    return jax.shard_map(local, mesh=mesh, in_specs=in_specs, out_specs=out_specs, check_vma=False)
```

```python
import functools

import jax
import jax.numpy as jnp
from jax import lax
from jax.experimental import pallas as pl
from jax.experimental.pallas import tpu as pltpu
from jax.sharding import PartitionSpec as P

BLOCK = 32
LEVELS = 8
LANES = 128
SMALLEST = 2.0**-40
F32, BF16 = jnp.float32, jnp.bfloat16

SETTINGS = pltpu.CompilerParams(vmem_limit_bytes=8 * 1024 * 1024)

FIRST = 5
RUN = 4
MIDDLE = 5

target_rms = 0.2
outer_rate = 0.7
outer_mu = 0.9


def spread_matrix(value):
    source = lax.broadcasted_iota(jnp.int32, (LANES, LANES), 0)
    target = lax.broadcasted_iota(jnp.int32, (LANES, LANES), 1)
    return jnp.where(source == (target | (BLOCK - 1)), value, 0.0).astype(BF16)


def quantized(values, jitter, strides):
    size = jnp.maximum(jnp.abs(values), SMALLEST) * (2.0 - 2.0**-23)
    widened = size * (2.0**23 + 1.0)
    ceiling = (widened - widened * (1.0 - 2.0**-24)).astype(BF16)
    step = 1
    for stride in strides:
        rolled = [pltpu.roll(ceiling, step * i, 1) for i in range(1, stride)]
        ceiling = functools.reduce(jnp.maximum, rolled, ceiling)
        step *= stride
    inverse = pl.reciprocal(ceiling.astype(F32), approx=True).astype(BF16)
    quantum = jnp.dot(ceiling, spread_matrix(1.0 / LEVELS), preferred_element_type=F32)
    inverse = jnp.dot(inverse, spread_matrix(1.0 * LEVELS), preferred_element_type=F32)
    scaled = values * inverse
    lower = jnp.floor(scaled)
    bumped = jnp.where(scaled - lower > jitter, lower + 1.0, lower)
    return (bumped * quantum).astype(BF16)


def first_kernel(own, group, values_hbm, jitter_hbm, second_hbm, out_ref, second_ref, values, jitter, done):
    place = pl.multiple_of(lax.rem(lax.axis_index("rep") + group - FIRST, group) * own, own)
    copies = [
        pltpu.make_async_copy(values_hbm, values, done.at[0]),
        pltpu.make_async_copy(jitter_hbm, jitter, done.at[1]),
        pltpu.make_async_copy(second_hbm.at[pl.ds(place, own)], second_ref, done.at[2]),
    ]
    for copy in copies:
        copy.start()
    copies[0].wait()
    copies[1].wait()
    out_ref[...] = quantized(values[...], jitter[...], (4, 2, 2, 2))
    copies[2].wait()


def partial_kernel(terms_ref, out_ref):
    total = terms_ref[0].astype(F32)
    for r in range(1, terms_ref.shape[0]):
        total = total + terms_ref[r].astype(F32)
    out_ref[...] = total


def second_kernel(reps, near_ref, far_ref, jitter_ref, out_ref):
    average = (near_ref[...] + far_ref[...]) * (1.0 / reps)
    grad = quantized(average, jitter_ref[...], (4, 8))
    for r in range(out_ref.shape[0]):
        out_ref[r] = grad


def square_kernel(grad_ref, out_ref):
    grad = grad_ref[...].astype(F32)
    out_ref[...] = jnp.broadcast_to(jnp.sum(grad * grad, axis=0, keepdims=True), out_ref.shape)


def update_kernel(full_count, chunks, squares_ref, grad_ref, params_ref, momentum_ref, new_params_hbm, new_momentum_hbm, new_params, new_momentum, done):
    squares = jnp.sum(squares_ref[...], keepdims=True)
    factor = target_rms * lax.rsqrt(squares * (1.0 / full_count) + 1e-06)
    rows = grad_ref.shape[0] // chunks
    copies = []
    for i in range(chunks):
        part = pl.ds(i * rows, rows)
        update = factor * grad_ref[part].astype(F32)
        moment = outer_mu * momentum_ref[part] + update
        new_momentum[part] = moment
        new_params[part] = params_ref[part] - outer_rate * (update + outer_mu * moment)
        copies += [
            pltpu.make_async_copy(new_momentum.at[part], new_momentum_hbm.at[part], done.at[0, i]),
            pltpu.make_async_copy(new_params.at[part], new_params_hbm.at[part], done.at[1, i]),
        ]
        copies[-2].start()
        copies[-1].start()
    for copy in copies:
        copy.wait()


def scalar_groups(reps, shards):
    groups = []
    for even in range(0, reps, 2):
        odd = even + 1
        one = MIDDLE * RUN + (RUN // 2 if even < reps // 2 else RUN // 2 - 1)
        two = one + RUN
        groups.append([odd * shards + one] + [even * shards + f for f in range(shards) if f != one])
        rest = [(even if f == one else odd) * shards + f for f in range(shards) if f != two]
        groups.append([odd * shards + two] + rest)
    return groups


def call(kernel, shape, kind, name, *arrays):
    out = jax.ShapeDtypeStruct(shape, kind)
    return pl.pallas_call(kernel, out_shape=out, compiler_params=SETTINGS, name=name)(*arrays)


def local(deltas, noise_first, params, momentum, noise_second):
    length = params.shape[0]
    rows = length // LANES
    reps, shards = lax.axis_size("rep"), lax.axis_size("fsdp")
    near = reps // 2
    own = rows // near
    chunks = 4
    turned = [(k + FIRST) % near for k in range(near)]
    halves = [turned, [near + k for k in turned]]

    def exchanged(array):
        return lax.all_to_all(array, "rep", 0, 0, axis_index_groups=halves, tiled=True)

    in_hbm = [
        pltpu.with_memory_space_constraint(array.reshape(rows, LANES), pltpu.HBM)
        for array in (deltas, noise_first, noise_second)
    ]
    terms, jitter = pl.pallas_call(
        functools.partial(first_kernel, own, near),
        in_specs=[pl.BlockSpec(memory_space=pltpu.HBM)] * 3,
        out_specs=[pl.BlockSpec(memory_space=pltpu.VMEM)] * 2,
        out_shape=[jax.ShapeDtypeStruct((rows, LANES), BF16), jax.ShapeDtypeStruct((own, LANES), F32)],
        scratch_shapes=[pltpu.VMEM((rows, LANES), F32)] * 2 + [pltpu.SemaphoreType.DMA((3,))],
        compiler_params=SETTINGS,
        name="quantize_first",
    )(*in_hbm)
    met = exchanged(terms.reshape(near, own, LANES))
    partial = call(partial_kernel, (own, LANES), F32, "partial", met)
    other = lax.ppermute(partial, "rep", [(r, (r + near) % reps) for r in range(reps)])
    second = functools.partial(second_kernel, reps)
    copies = call(second, (near, own, LANES), BF16, "quantize_second", partial, other, jitter)
    grad = exchanged(copies).reshape(rows, LANES)
    squares = call(square_kernel, (shards, LANES), F32, "squares", grad)
    groups = scalar_groups(reps, shards)
    squares = squares.reshape(shards, 1, LANES)
    squares = lax.all_to_all(squares, ("rep", "fsdp"), 0, 0, axis_index_groups=groups, tiled=True)

    new_params, new_momentum = pl.pallas_call(
        functools.partial(update_kernel, length * shards, chunks),
        in_specs=[pl.BlockSpec(memory_space=pltpu.VMEM)] * 4,
        out_specs=[pl.BlockSpec(memory_space=pltpu.HBM)] * 2,
        out_shape=[jax.ShapeDtypeStruct((rows, LANES), F32)] * 2,
        scratch_shapes=[pltpu.VMEM((rows, LANES), F32)] * 2 + [pltpu.SemaphoreType.DMA((2, chunks))],
        compiler_params=SETTINGS,
        name="update",
    )(squares.reshape(shards, LANES), grad, params.reshape(rows, LANES), momentum.reshape(rows, LANES))
    return new_params.reshape(length), new_momentum.reshape(length)


def solution(mesh):
    in_specs = (P("rep", "fsdp"), P("rep", "fsdp"), P("fsdp"), P("fsdp"), P("fsdp"))
    out_specs = (P("fsdp"), P("fsdp"))
    return jax.shard_map(local, mesh=mesh, in_specs=in_specs, out_specs=out_specs, check_vma=False)
```

```python
import functools

import jax
import jax.numpy as jnp
from jax import lax
from jax.experimental import pallas as pl
from jax.experimental.pallas import tpu as pltpu
from jax.sharding import PartitionSpec as P

BLOCK = 32
LEVELS = 8
LANES = 128
SMALLEST = 2.0**-40
F32, BF16 = jnp.float32, jnp.bfloat16

SETTINGS = pltpu.CompilerParams(vmem_limit_bytes=8 * 1024 * 1024)

FIRST = 5
RUN = 4

target_rms = 0.2
outer_rate = 0.7
outer_mu = 0.9


def spread_matrix(value):
    source = lax.broadcasted_iota(jnp.int32, (LANES, LANES), 0)
    target = lax.broadcasted_iota(jnp.int32, (LANES, LANES), 1)
    return jnp.where(source == (target | (BLOCK - 1)), value, 0.0).astype(BF16)


def quantized(values, jitter, strides):
    size = jnp.maximum(jnp.abs(values), SMALLEST) * (2.0 - 2.0**-23)
    widened = size * (2.0**23 + 1.0)
    ceiling = (widened - widened * (1.0 - 2.0**-24)).astype(BF16)
    step = 1
    for stride in strides:
        rolled = [pltpu.roll(ceiling, step * i, 1) for i in range(1, stride)]
        ceiling = functools.reduce(jnp.maximum, rolled, ceiling)
        step *= stride
    inverse = pl.reciprocal(ceiling.astype(F32), approx=True).astype(BF16)
    quantum = jnp.dot(ceiling, spread_matrix(1.0 / LEVELS), preferred_element_type=F32)
    inverse = jnp.dot(inverse, spread_matrix(1.0 * LEVELS), preferred_element_type=F32)
    scaled = values * inverse
    lower = jnp.floor(scaled)
    bumped = jnp.where(scaled - lower > jitter, lower + 1.0, lower)
    return (bumped * quantum).astype(BF16)


def first_kernel(own, group, values_hbm, jitter_hbm, second_hbm, out_ref, second_ref, values, jitter, done):
    place = pl.multiple_of(lax.rem(lax.axis_index("rep") + group - FIRST, group) * own, own)
    copies = [
        pltpu.make_async_copy(values_hbm, values, done.at[0]),
        pltpu.make_async_copy(jitter_hbm, jitter, done.at[1]),
        pltpu.make_async_copy(second_hbm.at[pl.ds(place, own)], second_ref, done.at[2]),
    ]
    for copy in copies:
        copy.start()
    for copy in copies:
        copy.wait()
    out_ref[...] = quantized(values[...], jitter[...], (2, 2, 2, 2, 2))


def partial_kernel(terms_ref, out_ref):
    total = terms_ref[0].astype(F32)
    for r in range(1, terms_ref.shape[0]):
        total = total + terms_ref[r].astype(F32)
    out_ref[...] = total


def second_kernel(reps, near_ref, far_ref, jitter_ref, out_ref):
    average = (near_ref[...] + far_ref[...]) * (1.0 / reps)
    grad = quantized(average, jitter_ref[...], (4, 8))
    for r in range(out_ref.shape[0]):
        out_ref[r] = grad


def square_kernel(grad_ref, out_ref):
    grad = grad_ref[...].astype(F32)
    out_ref[...] = jnp.broadcast_to(jnp.sum(grad * grad, axis=0, keepdims=True), out_ref.shape)


def update_kernel(full_count, chunks, squares_ref, grad_ref, params_ref, momentum_ref, new_params_hbm, new_momentum_hbm, new_params, new_momentum, done):
    squares = jnp.sum(squares_ref[...], keepdims=True)
    factor = target_rms * lax.rsqrt(squares * (1.0 / full_count) + 1e-06)
    rows = grad_ref.shape[0] // chunks
    copies = []
    for i in range(chunks):
        part = pl.ds(i * rows, rows)
        update = factor * grad_ref[part].astype(F32)
        moment = outer_mu * momentum_ref[part] + update
        new_momentum[part] = moment
        new_params[part] = params_ref[part] - outer_rate * (update + outer_mu * moment)
        copies += [
            pltpu.make_async_copy(new_momentum.at[part], new_momentum_hbm.at[part], done.at[0, i]),
            pltpu.make_async_copy(new_params.at[part], new_params_hbm.at[part], done.at[1, i]),
        ]
        copies[-2].start()
        copies[-1].start()
    for copy in copies:
        copy.wait()


def scalar_groups(reps, shards):
    groups = []
    for even in range(0, reps, 2):
        odd = even + 1
        one = shards - RUN + (RUN // 2 if even < reps // 2 else RUN // 2 - 1)
        two = one + (-1 if even < reps // 2 else 1)
        groups.append([odd * shards + one] + [even * shards + f for f in range(shards) if f != one])
        rest = [(even if f == one else odd) * shards + f for f in range(shards) if f != two]
        groups.append([odd * shards + two] + rest)
    return groups


def call(kernel, shape, kind, name, *arrays):
    out = jax.ShapeDtypeStruct(shape, kind)
    return pl.pallas_call(kernel, out_shape=out, compiler_params=SETTINGS, name=name)(*arrays)


def local(deltas, noise_first, params, momentum, noise_second):
    length = params.shape[0]
    rows = length // LANES
    reps, shards = lax.axis_size("rep"), lax.axis_size("fsdp")
    near = reps // 2
    own = rows // near
    chunks = 4
    turned = [(k + FIRST) % near for k in range(near)]
    halves = [turned, [near + k for k in turned]]

    def exchanged(array):
        return lax.all_to_all(array, "rep", 0, 0, axis_index_groups=halves, tiled=True)

    in_hbm = [
        pltpu.with_memory_space_constraint(array.reshape(rows, LANES), pltpu.HBM)
        for array in (deltas, noise_first, noise_second)
    ]
    terms, jitter = pl.pallas_call(
        functools.partial(first_kernel, own, near),
        in_specs=[pl.BlockSpec(memory_space=pltpu.HBM)] * 3,
        out_specs=[pl.BlockSpec(memory_space=pltpu.VMEM)] * 2,
        out_shape=[jax.ShapeDtypeStruct((rows, LANES), BF16), jax.ShapeDtypeStruct((own, LANES), F32)],
        scratch_shapes=[pltpu.VMEM((rows, LANES), F32)] * 2 + [pltpu.SemaphoreType.DMA((3,))],
        compiler_params=SETTINGS,
        name="quantize_first",
    )(*in_hbm)
    met = exchanged(terms.reshape(near, own, LANES))
    partial = call(partial_kernel, (own, LANES), F32, "partial", met)
    other = lax.ppermute(partial, "rep", [(r, (r + near) % reps) for r in range(reps)])
    second = functools.partial(second_kernel, reps)
    copies = call(second, (near, own, LANES), BF16, "quantize_second", partial, other, jitter)
    grad = exchanged(copies).reshape(rows, LANES)
    squares = call(square_kernel, (shards, LANES), F32, "squares", grad)
    groups = scalar_groups(reps, shards)
    squares = squares.reshape(shards, 1, LANES)
    squares = lax.all_to_all(squares, ("rep", "fsdp"), 0, 0, axis_index_groups=groups, tiled=True)

    new_params, new_momentum = pl.pallas_call(
        functools.partial(update_kernel, length * shards, chunks),
        in_specs=[pl.BlockSpec(memory_space=pltpu.VMEM)] * 4,
        out_specs=[pl.BlockSpec(memory_space=pltpu.HBM)] * 2,
        out_shape=[jax.ShapeDtypeStruct((rows, LANES), F32)] * 2,
        scratch_shapes=[pltpu.VMEM((rows, LANES), F32)] * 2 + [pltpu.SemaphoreType.DMA((2, chunks))],
        compiler_params=SETTINGS,
        name="update",
    )(squares.reshape(shards, LANES), grad, params.reshape(rows, LANES), momentum.reshape(rows, LANES))
    return new_params.reshape(length), new_momentum.reshape(length)


def solution(mesh):
    in_specs = (P("rep", "fsdp"), P("rep", "fsdp"), P("fsdp"), P("fsdp"), P("fsdp"))
    out_specs = (P("fsdp"), P("fsdp"))
    return jax.shard_map(local, mesh=mesh, in_specs=in_specs, out_specs=out_specs, check_vma=False)
```

```python
import functools

import jax
import jax.numpy as jnp
from jax import lax
from jax.experimental import pallas as pl
from jax.experimental.pallas import tpu as pltpu
from jax.sharding import PartitionSpec as P

BLOCK = 32
LEVELS = 8
LANES = 128
SMALLEST = 2.0**-40
F32, BF16 = jnp.float32, jnp.bfloat16

SETTINGS = pltpu.CompilerParams(vmem_limit_bytes=8 * 1024 * 1024)

FIRST = 5
RUN = 4

target_rms = 0.2
outer_rate = 0.7
outer_mu = 0.9


def spread_matrix(value):
    source = lax.broadcasted_iota(jnp.int32, (LANES, LANES), 0)
    target = lax.broadcasted_iota(jnp.int32, (LANES, LANES), 1)
    return jnp.where(source == (target | (BLOCK - 1)), value, 0.0).astype(BF16)


def quantized(values, jitter, strides):
    size = jnp.maximum(jnp.abs(values), SMALLEST) * (2.0 - 2.0**-23)
    widened = size * (2.0**23 + 1.0)
    ceiling = (widened - widened * (1.0 - 2.0**-24)).astype(BF16)
    step = 1
    for stride in strides:
        rolled = [pltpu.roll(ceiling, step * i, 1) for i in range(1, stride)]
        ceiling = functools.reduce(jnp.maximum, rolled, ceiling)
        step *= stride
    inverse = pl.reciprocal(ceiling.astype(F32), approx=True).astype(BF16)
    quantum = jnp.dot(ceiling, spread_matrix(1.0 / LEVELS), preferred_element_type=F32)
    inverse = jnp.dot(inverse, spread_matrix(1.0 * LEVELS), preferred_element_type=F32)
    scaled = values * inverse
    lower = jnp.floor(scaled)
    bumped = jnp.where(scaled - lower > jitter, lower + 1.0, lower)
    return (bumped * quantum).astype(BF16)


def first_kernel(own, group, values_hbm, jitter_hbm, second_hbm, out_ref, second_ref, values, jitter, done):
    place = pl.multiple_of(lax.rem(lax.axis_index("rep") + group - FIRST, group) * own, own)
    copies = [
        pltpu.make_async_copy(values_hbm, values, done.at[0]),
        pltpu.make_async_copy(jitter_hbm, jitter, done.at[1]),
        pltpu.make_async_copy(second_hbm.at[pl.ds(place, own)], second_ref, done.at[2]),
    ]
    for copy in copies:
        copy.start()
    for copy in copies:
        copy.wait()
    out_ref[...] = quantized(values[...], jitter[...], (2, 2, 2, 2, 2))


def partial_kernel(terms_ref, out_ref):
    total = terms_ref[0].astype(F32)
    for r in range(1, terms_ref.shape[0]):
        total = total + terms_ref[r].astype(F32)
    out_ref[...] = total


def second_kernel(reps, near_ref, far_ref, jitter_ref, out_ref):
    average = (near_ref[...] + far_ref[...]) * (1.0 / reps)
    grad = quantized(average, jitter_ref[...], (4, 8))
    for r in range(out_ref.shape[0]):
        out_ref[r] = grad


def square_kernel(grad_ref, out_ref):
    grad = grad_ref[...].astype(F32)
    out_ref[...] = jnp.broadcast_to(jnp.sum(grad * grad, axis=0, keepdims=True), out_ref.shape)


def update_kernel(full_count, chunks, squares_ref, grad_ref, params_ref, momentum_ref, new_params_hbm, new_momentum_hbm, new_params, new_momentum, done):
    squares = jnp.sum(squares_ref[...], keepdims=True)
    factor = target_rms * lax.rsqrt(squares * (1.0 / full_count) + 1e-06)
    rows = grad_ref.shape[0] // chunks
    copies = []
    for i in range(chunks):
        part = pl.ds(i * rows, rows)
        update = factor * grad_ref[part].astype(F32)
        moment = outer_mu * momentum_ref[part] + update
        new_momentum[part] = moment
        new_params[part] = params_ref[part] - outer_rate * (update + outer_mu * moment)
        copies += [
            pltpu.make_async_copy(new_momentum.at[part], new_momentum_hbm.at[part], done.at[0, i]),
            pltpu.make_async_copy(new_params.at[part], new_params_hbm.at[part], done.at[1, i]),
        ]
        copies[-2].start()
        copies[-1].start()
    for copy in copies:
        copy.wait()


def scalar_groups(reps, shards):
    groups = []
    for even in range(0, reps, 2):
        odd = even + 1
        one = shards - RUN + (RUN // 2 if even < reps // 2 else RUN // 2 - 1)
        two = one - RUN
        groups.append([odd * shards + one] + [even * shards + f for f in range(shards) if f != one])
        rest = [(even if f == one else odd) * shards + f for f in range(shards) if f != two]
        groups.append([odd * shards + two] + rest)
    return groups


def call(kernel, shape, kind, name, *arrays):
    out = jax.ShapeDtypeStruct(shape, kind)
    return pl.pallas_call(kernel, out_shape=out, compiler_params=SETTINGS, name=name)(*arrays)


def local(deltas, noise_first, params, momentum, noise_second):
    length = params.shape[0]
    rows = length // LANES
    reps, shards = lax.axis_size("rep"), lax.axis_size("fsdp")
    near = reps // 2
    own = rows // near
    chunks = 2
    turned = [(k + FIRST) % near for k in range(near)]
    halves = [turned, [near + k for k in turned]]

    def exchanged(array):
        return lax.all_to_all(array, "rep", 0, 0, axis_index_groups=halves, tiled=True)

    in_hbm = [
        pltpu.with_memory_space_constraint(array.reshape(rows, LANES), pltpu.HBM)
        for array in (deltas, noise_first, noise_second)
    ]
    terms, jitter = pl.pallas_call(
        functools.partial(first_kernel, own, near),
        in_specs=[pl.BlockSpec(memory_space=pltpu.HBM)] * 3,
        out_specs=[pl.BlockSpec(memory_space=pltpu.VMEM)] * 2,
        out_shape=[jax.ShapeDtypeStruct((rows, LANES), BF16), jax.ShapeDtypeStruct((own, LANES), F32)],
        scratch_shapes=[pltpu.VMEM((rows, LANES), F32)] * 2 + [pltpu.SemaphoreType.DMA((3,))],
        compiler_params=SETTINGS,
        name="quantize_first",
    )(*in_hbm)
    met = exchanged(terms.reshape(near, own, LANES))
    partial = call(partial_kernel, (own, LANES), F32, "partial", met)
    other = lax.ppermute(partial, "rep", [(r, (r + near) % reps) for r in range(reps)])
    second = functools.partial(second_kernel, reps)
    copies = call(second, (near, own, LANES), BF16, "quantize_second", partial, other, jitter)
    grad = exchanged(copies).reshape(rows, LANES)
    squares = call(square_kernel, (shards, LANES), F32, "squares", grad)
    groups = scalar_groups(reps, shards)
    squares = squares.reshape(shards, 1, LANES)
    squares = lax.all_to_all(squares, ("rep", "fsdp"), 0, 0, axis_index_groups=groups, tiled=True)

    new_params, new_momentum = pl.pallas_call(
        functools.partial(update_kernel, length * shards, chunks),
        in_specs=[pl.BlockSpec(memory_space=pltpu.VMEM)] * 4,
        out_specs=[pl.BlockSpec(memory_space=pltpu.HBM)] * 2,
        out_shape=[jax.ShapeDtypeStruct((rows, LANES), F32)] * 2,
        scratch_shapes=[pltpu.VMEM((rows, LANES), F32)] * 2 + [pltpu.SemaphoreType.DMA((2, chunks))],
        compiler_params=SETTINGS,
        name="update",
    )(squares.reshape(shards, LANES), grad, params.reshape(rows, LANES), momentum.reshape(rows, LANES))
    return new_params.reshape(length), new_momentum.reshape(length)


def solution(mesh):
    in_specs = (P("rep", "fsdp"), P("rep", "fsdp"), P("fsdp"), P("fsdp"), P("fsdp"))
    out_specs = (P("fsdp"), P("fsdp"))
    return jax.shard_map(local, mesh=mesh, in_specs=in_specs, out_specs=out_specs, check_vma=False)
```
